32 devices in a mesh: groups: 2 (over y), blk: 4 (over z), help: 4 (over x, core).
Axes of the slice: x: 2, y: 2, z: 4, core: 2. Of those that a mesh axis runs over, the one named last changes fastest.
Arguments:
- users: float32 [16384, 128], P(('groups', 'blk', 'help')), parts along dimension 0, may hold values from -2.5 to 2.5
- items: float32 [16384, 128], P(('groups', 'blk', 'help')), parts along dimension 0, may hold values from -2.5 to 2.5
- user_state: float32 [16384], P(('groups', 'blk', 'help')), parts along dimension 0, may hold values from 5 to 50
- item_state: float32 [16384], P(('groups', 'blk', 'help')), parts along dimension 0, may hold values from 5 to 50
- ratings: bfloat16 [8, 4, 2, 16, 128, 128], P(('groups', 'blk'), 'help'), parts along dimension 0
- masks: bfloat16 [8, 4, 2, 16, 128, 128], P(('groups', 'blk'), 'help'), parts along dimension 0, may hold values from 0 to 2, as said below
- tile_cells: int32 [8, 4, 2, 16], P(('groups', 'blk'), 'help'), parts along dimension 0, may hold values from 0 to 15, as said below
- tile_count: int32 [8, 4, 2], P(('groups', 'blk'), 'help'), parts along dimension 0, may hold values from 1 to 16, as said below
Outputs:
- users_out: float32 [16384, 128], P(('groups', 'blk', 'help')), parts along dimension 0
- items_out: float32 [16384, 128], P(('groups', 'blk', 'help')), parts along dimension 0
- user_state_out: float32 [16384], P(('groups', 'blk', 'help')), parts along dimension 0
- item_state_out: float32 [16384], P(('groups', 'blk', 'help')), parts along dimension 0
- loss: float32 [2], P('groups'), parts along dimension 0
The draws below stay inside these ranges and needn't reach their ends.
There are 2 independent parts, one for each index of `groups`. The reference program is written for one: setup_inputs(seed, part) draws one part's arguments, and reference() takes and returns one part's arrays. A program takes and returns all parts, laid end to end along the dimension named above; each array names one. Nothing has to cross between parts.
Inputs may be any that keep to these rules, and one draw needn't show every extreme that they name: `tile_cells`: slots are in any order; each user tile and item tile pair of a stratum appears in exactly one slot. `tile_count`: some position of each draw has all 16 slots live. `masks`: entries of slots at or past the live count are zero; unrated entries are zero.
All inputs are finite; a program needn't handle non-finite values.
Results may differ from the reference program's by a relative error of at most 0.0016.
Values may be sent and summed in bfloat16 or wider, within the bound.
A program may use at most 64 MiB of HBM per device.

```python
import math
import jax
import jax.numpy as jnp
from jax import lax

R = 128
TILE = 128
UT = 4
IT = 4
SUBS = 2
INNER = 2
TCAP = 16
USERS = 8192
ITEMS = 8192
N_BLK = 4
N_HELP = 4


def live_counts(key):
    first, second, third = jax.random.split(jax.random.fold_in(key, 101), 3)
    shape = (N_BLK, N_HELP, SUBS)
    heavy = jax.random.randint(first, shape, 0, 8) == 0
    base = jax.random.randint(second, shape, max(1, TCAP // 8), TCAP // 2 + 1)
    chosen = jax.random.randint(third, (), 0, N_BLK * N_HELP)
    flat = jnp.arange(N_BLK * N_HELP, dtype=jnp.int32).reshape(N_BLK, N_HELP, 1)
    return jnp.where(heavy | (flat == chosen), TCAP, base).astype(jnp.int32)


def draw_tile_count(key, part):
    return live_counts(key)


def draw_masks(key, part):
    counts = live_counts(key)
    key = jax.random.fold_in(key, 7)
    rated_key, value_key = jax.random.split(key)
    shape = (N_BLK, N_HELP, SUBS, TCAP, TILE, TILE)
    rated = jax.random.randint(rated_key, shape, 0, 5) < 3
    values = jax.random.uniform(value_key, shape, jnp.float32, 0.5, 1.5)
    slots = jnp.arange(TCAP, dtype=jnp.int32).reshape(1, 1, 1, TCAP, 1, 1)
    live = slots < counts[:, :, :, None, None, None]
    return jnp.where(live & rated, values, 0.0).astype(jnp.bfloat16)


def draw_tile_cells(key, part):
    key = jax.random.fold_in(key, 3)
    scores = jax.random.randint(key, (N_BLK, N_HELP, SUBS, TCAP), 0, 1048576) * TCAP
    scores = scores + jnp.arange(TCAP, dtype=jnp.int32)
    return jnp.argsort(scores, axis=-1, stable=True).astype(jnp.int32)


def draw_ratings(key, part):
    key = jax.random.fold_in(key, 5)
    shape = (N_BLK, N_HELP, SUBS, TCAP, TILE, TILE)
    ramp = jnp.arange(N_BLK, dtype=jnp.float32) / max(N_BLK - 1, 1)
    values = jax.random.normal(key, shape, jnp.float32)
    scale = 0.6 + 1.2 * ramp
    return (values * scale.reshape(N_BLK, 1, 1, 1, 1, 1)).astype(jnp.bfloat16)


def levels(key, shape, pieces, smallest, largest):
    level, own = 1.0, jax.random.fold_in(key, 6)
    for dim, parts in pieces:
        heights = jnp.exp(jax.random.uniform(jax.random.fold_in(own, dim), (parts,), jnp.float32, smallest / len(pieces), largest / len(pieces)))
        level = level * jnp.repeat(heights, shape[dim] // parts).reshape([-1 if axis == dim else 1 for axis in range(len(shape))])
    return level


def gaussian(key, dims, scale, limit, pieces=(), kind=jnp.bfloat16):
    drawn = jax.random.normal(key, dims, jnp.float32) * scale
    if len(pieces) > 0:
        drawn = levels(key, dims, pieces, -0.22, 0.18) * drawn
    return jnp.clip(drawn, min=-limit, max=limit).astype(kind)


def setup_inputs(seed: int = 0, part: int = 0) -> dict:
    key_of = jax.random.split(jax.random.key(seed), 9)
    part_keys = jax.random.split(jax.random.fold_in(key_of[8], part), 9)
    return {
        "users": gaussian(part_keys[0], (USERS, R), 0.3, 2.5, ((0, 16),), jnp.float32),
        "items": gaussian(part_keys[1], (ITEMS, R), 0.3, 2.5, ((0, 16),), jnp.float32),
        "user_state": jnp.clip(jnp.exp(math.log(50.0) - 2.3025851 * jax.random.uniform(part_keys[2], (USERS,), jnp.float32) ** levels(part_keys[2], (USERS,), ((0, 16),), -0.2, 0.2)), 5.0, 50.0),
        "item_state": jnp.clip(jnp.exp(math.log(50.0) - 2.3025851 * jax.random.uniform(part_keys[3], (ITEMS,), jnp.float32) ** levels(part_keys[3], (ITEMS,), ((0, 16),), -0.2, 0.2)), 5.0, 50.0),
        "ratings": draw_ratings(jax.random.fold_in(jax.random.fold_in(key_of[8], part), 71), part),
        "masks": draw_masks(jax.random.fold_in(jax.random.fold_in(key_of[8], part), 71), part),
        "tile_cells": draw_tile_cells(jax.random.fold_in(jax.random.fold_in(key_of[8], part), 71), part),
        "tile_count": draw_tile_count(jax.random.fold_in(jax.random.fold_in(key_of[8], part), 71), part),
    }


EPS = 1e-06
LEARN = 0.03
DECAY = 0.02

def tile_terms(users_narrow, items_narrow, ratings, masks, cells, live):
    user_grid = users_narrow.reshape(UT, TILE, R)
    item_grid = items_narrow.reshape(IT, TILE, R)
    user_ids = cells // IT
    item_ids = cells % IT
    slots = jnp.arange(TCAP, dtype=jnp.int32)
    weight = masks.astype(jnp.float32) * (slots < live).astype(jnp.float32)[:, None, None]
    user_part = jnp.take(user_grid, user_ids, axis=0).astype(jnp.float32)
    item_part = jnp.take(item_grid, item_ids, axis=0).astype(jnp.float32)
    predicted = jnp.einsum('tar,tbr->tab', user_part, item_part, precision=lax.Precision.HIGHEST)
    error = weight * (predicted - ratings.astype(jnp.float32))
    error_narrow = lax.optimization_barrier(error.astype(jnp.bfloat16)).astype(jnp.float32)
    user_terms = jnp.einsum('tab,tbr->tar', error_narrow, item_part, precision=lax.Precision.HIGHEST)
    item_terms = jnp.einsum('tab,tar->tbr', error_narrow, user_part, precision=lax.Precision.HIGHEST)
    user_onehot = (user_ids[:, None] == jnp.arange(UT, dtype=jnp.int32)[None, :]).astype(jnp.float32)
    item_onehot = (item_ids[:, None] == jnp.arange(IT, dtype=jnp.int32)[None, :]).astype(jnp.float32)
    grad_users = jnp.einsum('tk,tar->kar', user_onehot, user_terms, precision=lax.Precision.HIGHEST)
    grad_items = jnp.einsum('tk,tbr->kbr', item_onehot, item_terms, precision=lax.Precision.HIGHEST)
    return (grad_users, grad_items, jnp.sum(error * error), jnp.sum(weight))

def adagrad(factors, state, grads):
    state_new = state + lax.optimization_barrier(jnp.mean(grads * grads, axis=-1))
    return (factors - LEARN * grads / jnp.sqrt(state_new + EPS)[:, None], state_new)

def device_pass(carry):
    users, items, user_state, item_state, ratings, masks, cells, live = carry
    squared = jnp.float32(0.0)
    counted = jnp.float32(0.0)
    for inner in range(INNER):
        grad_users, grad_items, part_sq, part_count = tile_terms(users.astype(jnp.bfloat16), items.astype(jnp.bfloat16), ratings, masks, cells, live)
        squared = squared + part_sq
        counted = counted + part_count
        grad_users = grad_users.reshape(users.shape) + DECAY * users
        grad_items = grad_items.reshape(items.shape) + DECAY * items
        users, user_state = adagrad(users, user_state, grad_users)
        items, item_state = adagrad(items, item_state, grad_items)
    return (users, items, user_state, item_state, squared, counted)

def reference(users, items, user_state, item_state, ratings, masks, tile_cells, tile_count):
    places = N_BLK * N_HELP
    users = users.reshape(places, UT * TILE, R)
    items = items.reshape(places, IT * TILE, R)
    user_state = user_state.reshape(places, UT * TILE)
    item_state = item_state.reshape(places, IT * TILE)
    squared = jnp.float32(0.0)
    counted = jnp.float32(0.0)
    for stratum in range(SUBS):
        outcome = lax.map(device_pass, (users, items, user_state, item_state, ratings[:, :, stratum].reshape(places, TCAP, TILE, TILE), masks[:, :, stratum].reshape(places, TCAP, TILE, TILE), tile_cells[:, :, stratum].reshape(places, TCAP), tile_count[:, :, stratum].reshape(places)))
        users, items, user_state, item_state = (outcome[0], outcome[1], outcome[2], outcome[3])
        squared = squared + jnp.sum(outcome[4])
        counted = counted + jnp.sum(outcome[5])
        items = jnp.roll(items.reshape(N_BLK, N_HELP, IT * TILE, R), 1, axis=0).reshape(places, IT * TILE, R)
        item_state = jnp.roll(item_state.reshape(N_BLK, N_HELP, IT * TILE), 1, axis=0).reshape(places, IT * TILE)
    loss = (squared / counted).reshape(1)
    return (users.reshape(USERS, R), items.reshape(ITEMS, R), user_state.reshape(USERS), item_state.reshape(ITEMS), loss)
```

```python
import functools

import jax
import jax.numpy as jnp
from jax import lax
from jax.experimental import pallas as pl
from jax.experimental.pallas import tpu as pltpu
from jax.sharding import PartitionSpec as P

INNER = 2
EPS = 1e-06
LEARN = 0.03
DECAY = 0.02
LEVELS = 32767.0
CHUNK = 256
MESH = pl.DeviceIdType.MESH
F32 = jnp.float32
BF16 = jnp.bfloat16


def inverse_cells(cells_ref, stratum, capacity):
    picked = [cells_ref[0, 0, stratum, slot] for slot in range(capacity)]
    where = []
    for cell in range(capacity):
        found = jnp.int32(0)
        for slot in range(1, capacity):
            found = jnp.where(picked[slot] == cell, jnp.int32(slot), found)
        where.append(found)
    return where


def encode(values):
    top = jnp.max(jnp.abs(values), axis=0, keepdims=True)
    scale = jnp.maximum(top, 1e-30) * (1.0 / LEVELS)
    codes = jnp.round(values * (1.0 / scale)).astype(jnp.int32).astype(jnp.int16)
    return codes, scale


def kernel(
    sizes,
    cells_ref, users_ref, items_ref, ustate_ref, istate_ref, ratings_ref, masks_ref,
    users_out, items_out, ustate_out, istate_out, loss_ref,
    users, items_nat, items, ustate_in, ustate_row, ustate, istate, error,
    items_back, codes_out, aux_out, codes_in, aux_in, sums_help, sums_blk,
    load_sem, store_sem, code_send, code_recv, aux_send, aux_recv,
    help_send, help_recv, blk_send, blk_recv, *tiles,
):
    strata, capacity, tile, rank, user_tiles, item_tiles, n_blk, n_help = sizes
    rat, msk = tiles[:strata], tiles[strata:]
    n_items = item_tiles * tile
    chunks = n_items // CHUNK
    per_chunk = CHUNK // tile
    my_blk = lax.axis_index("blk")
    my_help = lax.axis_index("help")
    right = lax.rem(my_blk + 1, n_blk)

    loads = {}
    plan = [("users", users_ref, users), ("items", items_ref, items_nat),
            ("ustate", ustate_ref, ustate_in), ("istate", istate_ref, istate)]
    for s in range(strata):
        plan.append((("m", s), masks_ref.at[0, 0, s], msk[s]))
        plan.append((("r", s), ratings_ref.at[0, 0, s], rat[s]))
    for number, (name, src, dst) in enumerate(plan):
        loads[name] = pltpu.make_async_copy(src, dst, load_sem.at[number])
        loads[name].start()

    barrier = pltpu.get_barrier_semaphore()
    for d in range(1, n_blk):
        pl.semaphore_signal(barrier, inc=1, device_id={"blk": lax.rem(my_blk + d, n_blk)}, device_id_type=MESH)
    for d in range(1, n_help):
        pl.semaphore_signal(barrier, inc=1, device_id={"help": lax.rem(my_help + d, n_help)}, device_id_type=MESH)

    slots = [inverse_cells(cells_ref, s, capacity) for s in range(strata)]

    loads["items"].wait()
    for i in range(item_tiles):
        items[:, i * tile:(i + 1) * tile] = items_nat[i * tile:(i + 1) * tile, :].T
    loads["istate"].wait()
    loads["ustate"].wait()
    for u in range(user_tiles):
        ustate[u * tile:(u + 1) * tile, :] = jnp.broadcast_to(ustate_in[u:u + 1, :], (tile, tile)).T
    loads["users"].wait()

    squared = jnp.zeros((8, tile), F32)
    counted = jnp.zeros((8, tile), F32)

    def shift(hop, c):
        cols = pl.ds(c * CHUNK, CHUNK)
        code = pltpu.make_async_remote_copy(
            src_ref=codes_out.at[hop, c], dst_ref=codes_in.at[hop, c],
            send_sem=code_send.at[hop, c], recv_sem=code_recv.at[hop, c],
            device_id={"blk": right}, device_id_type=MESH)
        aux = pltpu.make_async_remote_copy(
            src_ref=aux_out.at[hop, c], dst_ref=aux_in.at[hop, c],
            send_sem=aux_send.at[hop, c], recv_sem=aux_recv.at[hop, c],
            device_id={"blk": right}, device_id_type=MESH)
        return code, aux

    def fold(x):
        return x.reshape(-1, 8, tile).sum(axis=0)

    for s in range(strata):
        loads[("m", s)].wait()
        loads[("r", s)].wait()
        for inner in range(INNER):
            last = inner == INNER - 1
            un = [users[u * tile:(u + 1) * tile, :].astype(BF16) for u in range(user_tiles)]
            ut = jnp.concatenate([x.T for x in un], axis=1)
            for c in range(chunks):
                lo, hi = c * CHUNK, (c + 1) * CHUNK
                if s > 0 and inner == 0:
                    code, aux = shift(s - 1, c)
                    code.wait_recv()
                    aux.wait_recv()
                    block = codes_in[s - 1, c].astype(jnp.int32).astype(F32) * aux_in[s - 1, c, 0:1, :]
                    items[:, lo:hi] = block
                    istate[0:1, lo:hi] = aux_in[s - 1, c, 1:2, :]
                block = items[:, lo:hi]
                narrow = block.astype(BF16)
                for k in range(per_chunk):
                    items_back[lo + k * tile:lo + (k + 1) * tile, :] = narrow[:, k * tile:(k + 1) * tile].T
                for u in range(user_tiles):
                    predicted = jnp.dot(un[u], narrow, preferred_element_type=F32)
                    for k in range(per_chunk):
                        i = c * per_chunk + k
                        at = slots[s][u * item_tiles + i]
                        weight = msk[s][at].astype(F32)
                        err = weight * (predicted[:, k * tile:(k + 1) * tile] - rat[s][at].astype(F32))
                        squared = squared + fold(err * err)
                        if inner == 0:
                            counted = counted + fold(weight)
                        error[u * tile:(u + 1) * tile, i * tile:(i + 1) * tile] = err.astype(BF16)
                grad = jnp.dot(ut, error[:, lo:hi], preferred_element_type=F32) + DECAY * block
                state = istate[0:1, lo:hi] + jnp.sum(grad * grad, axis=0, keepdims=True) * (1.0 / rank)
                block = block - (LEARN * grad) * lax.rsqrt(state + EPS)
                if not last:
                    items[:, lo:hi] = block
                    istate[0:1, lo:hi] = state
                else:
                    codes, scale = encode(block)
                    codes_out[s, c] = codes
                    aux_out[s, c] = jnp.concatenate([scale, state] + [jnp.zeros_like(scale)] * 6, axis=0)
                    if s == 0 and c == 0:
                        pl.semaphore_wait(barrier, (n_blk - 1) + (n_help - 1))
                    for copy in shift(s, c):
                        copy.start()
            if s == strata - 1 and last:
                mine = jnp.concatenate(
                    [jnp.sum(squared, axis=0, keepdims=True),
                     jnp.sum(counted, axis=0, keepdims=True) * float(INNER),
                     jnp.zeros((6, tile), F32)], axis=0)
                sums_help[my_help] = mine
                helps = []
                for d in range(1, n_help):
                    helps.append(pltpu.make_async_remote_copy(
                        src_ref=sums_help.at[my_help], dst_ref=sums_help.at[my_help],
                        send_sem=help_send.at[d], recv_sem=help_recv.at[my_help],
                        device_id={"help": lax.rem(my_help + d, n_help)}, device_id_type=MESH))
                    helps[-1].start()
            for u in range(user_tiles):
                rows = slice(u * tile, (u + 1) * tile)
                own = users[rows, :]
                grad = jnp.dot(error[rows, :], items_back[...], preferred_element_type=F32) + DECAY * own
                state = ustate[rows, :] + jnp.sum(grad * grad, axis=1, keepdims=True) * (1.0 / rank)
                ustate[rows, :] = state
                users[rows, :] = own - (LEARN * grad) * lax.rsqrt(state + EPS)

    stores = [pltpu.make_async_copy(users, users_out, store_sem.at[0])]
    stores[-1].start()
    for u in range(user_tiles):
        ustate_row[u:u + 1, :] = ustate[u * tile:(u + 1) * tile, :].T[0:1, :]
    stores.append(pltpu.make_async_copy(ustate_row, ustate_out, store_sem.at[1]))
    stores[-1].start()

    def arrival(buf, axis, index, send, recv):
        return pltpu.make_async_remote_copy(
            src_ref=buf.at[index], dst_ref=buf.at[index], send_sem=send.at[0],
            recv_sem=recv.at[index], device_id={axis: index}, device_id_type=MESH)

    for d in range(1, n_help):
        arrival(sums_help, "help", lax.rem(my_help + d, n_help), help_send, help_recv).wait_recv()
    total = sums_help[0]
    for j in range(1, n_help):
        total = total + sums_help[j]
    sums_blk[my_blk] = total
    blks = []
    for d in range(1, n_blk):
        blks.append(pltpu.make_async_remote_copy(
            src_ref=sums_blk.at[my_blk], dst_ref=sums_blk.at[my_blk],
            send_sem=blk_send.at[d], recv_sem=blk_recv.at[my_blk],
            device_id={"blk": lax.rem(my_blk + d, n_blk)}, device_id_type=MESH))
        blks[-1].start()

    for c in range(chunks):
        lo = c * CHUNK
        code, aux = shift(strata - 1, c)
        code.wait_recv()
        aux.wait_recv()
        block = codes_in[strata - 1, c].astype(jnp.int32).astype(F32) * aux_in[strata - 1, c, 0:1, :]
        istate[0:1, lo:lo + CHUNK] = aux_in[strata - 1, c, 1:2, :]
        for k in range(per_chunk):
            items_nat[lo + k * tile:lo + (k + 1) * tile, :] = block[:, k * tile:(k + 1) * tile].T
        rows = pl.ds(lo, CHUNK)
        stores.append(pltpu.make_async_copy(items_nat.at[rows], items_out.at[rows], store_sem.at[3 + c]))
        stores[-1].start()
    stores.append(pltpu.make_async_copy(istate, istate_out, store_sem.at[2]))
    stores[-1].start()

    for d in range(1, n_blk):
        arrival(sums_blk, "blk", lax.rem(my_blk + d, n_blk), blk_send, blk_recv).wait_recv()
    total = sums_blk[0]
    for j in range(1, n_blk):
        total = total + sums_blk[j]
    loss_ref[0] = jnp.sum(total[0:1, :]) / jnp.sum(total[1:2, :])

    for copy in helps + blks:
        copy.wait_send()
    for hop in range(strata):
        for c in range(chunks):
            for copy in shift(hop, c):
                copy.wait_send()
    for copy in stores:
        copy.wait()


def on_device(users, items, user_state, item_state, ratings, masks, tile_cells, tile_count):
    strata, capacity, tile = ratings.shape[2], ratings.shape[3], ratings.shape[4]
    rank = users.shape[1]
    n_users, n_items = users.shape[0], items.shape[0]
    user_tiles, item_tiles = n_users // tile, n_items // tile
    n_blk, n_help = lax.axis_size("blk"), lax.axis_size("help")
    chunks = n_items // CHUNK
    sizes = (strata, capacity, tile, rank, user_tiles, item_tiles, n_blk, n_help)
    hbm = pl.BlockSpec(memory_space=pl.ANY)
    smem = pl.BlockSpec(memory_space=pltpu.SMEM)
    dma = pltpu.SemaphoreType.DMA
    outs = pl.pallas_call(
        functools.partial(kernel, sizes),
        out_shape=(
            jax.ShapeDtypeStruct(users.shape, F32),
            jax.ShapeDtypeStruct(items.shape, F32),
            jax.ShapeDtypeStruct((user_tiles, tile), F32),
            jax.ShapeDtypeStruct((1, n_items), F32),
            jax.ShapeDtypeStruct((1,), F32),
        ),
        in_specs=[smem] + [hbm] * 6,
        out_specs=(hbm, hbm, hbm, hbm, smem),
        scratch_shapes=[
            pltpu.VMEM((n_users, rank), F32),
            pltpu.VMEM((n_items, rank), F32),
            pltpu.VMEM((rank, n_items), F32),
            pltpu.VMEM((user_tiles, tile), F32),
            pltpu.VMEM((user_tiles, tile), F32),
            pltpu.VMEM((n_users, tile), F32),
            pltpu.VMEM((1, n_items), F32),
            pltpu.VMEM((n_users, n_items), BF16),
            pltpu.VMEM((n_items, rank), BF16),
            pltpu.VMEM((strata, chunks, rank, CHUNK), jnp.int16),
            pltpu.VMEM((strata, chunks, 8, CHUNK), F32),
            pltpu.VMEM((strata, chunks, rank, CHUNK), jnp.int16),
            pltpu.VMEM((strata, chunks, 8, CHUNK), F32),
            pltpu.VMEM((n_help, 8, tile), F32),
            pltpu.VMEM((n_blk, 8, tile), F32),
            dma((4 + 2 * strata,)),
            dma((3 + chunks,)),
            dma((strata, chunks)), dma((strata, chunks)),
            dma((strata, chunks)), dma((strata, chunks)),
            dma((n_help,)), dma((n_help,)),
            dma((n_blk,)), dma((n_blk,)),
        ] + [pltpu.VMEM((capacity, tile, tile), BF16)] * (2 * strata),
        compiler_params=pltpu.CompilerParams(
            collective_id=0, has_side_effects=True, vmem_limit_bytes=56 * 1024 * 1024
        ),
        name="block_steps",
    )(tile_cells, users, items, user_state.reshape(user_tiles, tile), item_state.reshape(1, n_items), ratings, masks)
    users_out, items_out, ustate_out, istate_out, loss = outs
    return users_out, items_out, ustate_out.reshape(n_users), istate_out.reshape(n_items), loss


def solution(mesh):
    in_specs = (
        P(("groups", "blk", "help"), None),
        P(("groups", "blk", "help"), None),
        P(("groups", "blk", "help")),
        P(("groups", "blk", "help")),
        P(("groups", "blk"), "help", None, None, None, None),
        P(("groups", "blk"), "help", None, None, None, None),
        P(("groups", "blk"), "help", None, None),
        P(("groups", "blk"), "help", None),
    )
    out_specs = (
        P(("groups", "blk", "help"), None),
        P(("groups", "blk", "help"), None),
        P(("groups", "blk", "help")),
        P(("groups", "blk", "help")),
        P("groups"),
    )
    return jax.shard_map(
        on_device, mesh=mesh, in_specs=in_specs, out_specs=out_specs, check_vma=False
    )
```

```python
import functools

import jax
import jax.numpy as jnp
from jax import lax
from jax.experimental import pallas as pl
from jax.experimental.pallas import tpu as pltpu
from jax.sharding import PartitionSpec as P

INNER = 2
EPS = 1e-06
LEARN = 0.03
DECAY = 0.02
LEVELS = 32767.0
CHUNK = 256
VMEM = 56 * 1024 * 1024
MESH = pl.DeviceIdType.MESH
F32 = jnp.float32
BF16 = jnp.bfloat16


def inverse_cells(cells_ref, stratum, capacity):
    picked = [cells_ref[0, 0, stratum, slot] for slot in range(capacity)]
    where = []
    for cell in range(capacity):
        found = jnp.int32(0)
        for slot in range(1, capacity):
            found = jnp.where(picked[slot] == cell, jnp.int32(slot), found)
        where.append(found)
    return where


def encode(values):
    top = jnp.max(jnp.abs(values), axis=0, keepdims=True)
    scale = jnp.maximum(top, 1e-30) * (1.0 / LEVELS)
    codes = jnp.round(values * (1.0 / scale)).astype(jnp.int32).astype(jnp.int16)
    return codes, scale


def kernel(
    sizes,
    cells_ref, users_ref, items_ref, ustate_ref, istate_ref, ratings_ref, masks_ref,
    users, items_nat, ustate_row, istate, loss_ref,
    items, ustate_in, ustate, error,
    items_back, codes_out, aux_out, codes_in, aux_in, sums_help, sums_blk,
    load_sem, code_send, code_recv, aux_send, aux_recv,
    help_send, help_recv, blk_send, blk_recv, *tiles,
):
    strata, capacity, tile, rank, user_tiles, item_tiles, n_blk, n_help = sizes
    rat, msk = tiles[:strata], tiles[strata:]
    n_items = item_tiles * tile
    chunks = n_items // CHUNK
    per_chunk = CHUNK // tile
    my_blk = lax.axis_index("blk")
    my_help = lax.axis_index("help")
    right = lax.rem(my_blk + 1, n_blk)

    loads = {}
    plan = [("users", users_ref, users), ("items", items_ref, items_nat),
            ("ustate", ustate_ref, ustate_in), ("istate", istate_ref, istate)]
    for s in range(strata):
        plan.append((("m", s), masks_ref.at[0, 0, s], msk[s]))
        plan.append((("r", s), ratings_ref.at[0, 0, s], rat[s]))
    for number, (name, src, dst) in enumerate(plan):
        loads[name] = pltpu.make_async_copy(src, dst, load_sem.at[number])
        loads[name].start()

    barrier = pltpu.get_barrier_semaphore()
    for d in range(1, n_blk):
        pl.semaphore_signal(barrier, inc=1, device_id={"blk": lax.rem(my_blk + d, n_blk)}, device_id_type=MESH)
    for d in range(1, n_help):
        pl.semaphore_signal(barrier, inc=1, device_id={"help": lax.rem(my_help + d, n_help)}, device_id_type=MESH)

    slots = [inverse_cells(cells_ref, s, capacity) for s in range(strata)]

    loads["items"].wait()
    for i in range(item_tiles):
        items[:, i * tile:(i + 1) * tile] = items_nat[i * tile:(i + 1) * tile, :].T
    loads["istate"].wait()
    loads["ustate"].wait()
    for u in range(user_tiles):
        ustate[u * tile:(u + 1) * tile, :] = jnp.broadcast_to(ustate_in[u:u + 1, :], (tile, tile)).T
    loads["users"].wait()

    squared = jnp.zeros((8, tile), F32)
    counted = jnp.zeros((8, tile), F32)

    def shift(hop, c):
        cols = pl.ds(c * CHUNK, CHUNK)
        code = pltpu.make_async_remote_copy(
            src_ref=codes_out.at[hop, c], dst_ref=codes_in.at[hop, c],
            send_sem=code_send.at[hop, c], recv_sem=code_recv.at[hop, c],
            device_id={"blk": right}, device_id_type=MESH)
        aux = pltpu.make_async_remote_copy(
            src_ref=aux_out.at[hop, c], dst_ref=aux_in.at[hop, c],
            send_sem=aux_send.at[hop, c], recv_sem=aux_recv.at[hop, c],
            device_id={"blk": right}, device_id_type=MESH)
        return code, aux

    def fold(x):
        return x.reshape(-1, 8, tile).sum(axis=0)

    for s in range(strata):
        loads[("m", s)].wait()
        loads[("r", s)].wait()
        for inner in range(INNER):
            last = inner == INNER - 1
            un = [users[u * tile:(u + 1) * tile, :].astype(BF16) for u in range(user_tiles)]
            ut = jnp.concatenate([x.T for x in un], axis=1)
            for c in range(chunks):
                lo, hi = c * CHUNK, (c + 1) * CHUNK
                if s > 0 and inner == 0:
                    code, aux = shift(s - 1, c)
                    code.wait_recv()
                    aux.wait_recv()
                    block = codes_in[s - 1, c].astype(jnp.int32).astype(F32) * aux_in[s - 1, c, 0:1, :]
                    items[:, lo:hi] = block
                    istate[0:1, lo:hi] = aux_in[s - 1, c, 1:2, :]
                block = items[:, lo:hi]
                narrow = block.astype(BF16)
                for k in range(per_chunk):
                    items_back[lo + k * tile:lo + (k + 1) * tile, :] = narrow[:, k * tile:(k + 1) * tile].T
                for u in range(user_tiles):
                    predicted = jnp.dot(un[u], narrow, preferred_element_type=F32)
                    for k in range(per_chunk):
                        i = c * per_chunk + k
                        at = slots[s][u * item_tiles + i]
                        weight = msk[s][at].astype(F32)
                        err = weight * (predicted[:, k * tile:(k + 1) * tile] - rat[s][at].astype(F32))
                        squared = squared + fold(err * err)
                        if inner == 0:
                            counted = counted + fold(weight)
                        error[u * tile:(u + 1) * tile, i * tile:(i + 1) * tile] = err.astype(BF16)
                grad = jnp.dot(ut, error[:, lo:hi], preferred_element_type=F32) + DECAY * block
                state = istate[0:1, lo:hi] + jnp.sum(grad * grad, axis=0, keepdims=True) * (1.0 / rank)
                block = block - (LEARN * grad) * lax.rsqrt(state + EPS)
                if not last:
                    items[:, lo:hi] = block
                    istate[0:1, lo:hi] = state
                else:
                    codes, scale = encode(block)
                    codes_out[s, c] = codes
                    aux_out[s, c] = jnp.concatenate([scale, state] + [jnp.zeros_like(scale)] * 6, axis=0)
                    if s == 0 and c == 0:
                        pl.semaphore_wait(barrier, (n_blk - 1) + (n_help - 1))
                    for copy in shift(s, c):
                        copy.start()
            if s == strata - 1 and last:
                mine = jnp.concatenate(
                    [jnp.sum(squared, axis=0, keepdims=True),
                     jnp.sum(counted, axis=0, keepdims=True) * float(INNER),
                     jnp.zeros((6, tile), F32)], axis=0)
                sums_help[my_help] = mine
                helps = []
                for d in range(1, n_help):
                    helps.append(pltpu.make_async_remote_copy(
                        src_ref=sums_help.at[my_help], dst_ref=sums_help.at[my_help],
                        send_sem=help_send.at[d], recv_sem=help_recv.at[my_help],
                        device_id={"help": lax.rem(my_help + d, n_help)}, device_id_type=MESH))
                    helps[-1].start()
            for u in range(user_tiles):
                rows = slice(u * tile, (u + 1) * tile)
                own = users[rows, :]
                grad = jnp.dot(error[rows, :], items_back[...], preferred_element_type=F32) + DECAY * own
                state = ustate[rows, :] + jnp.sum(grad * grad, axis=1, keepdims=True) * (1.0 / rank)
                ustate[rows, :] = state
                users[rows, :] = own - (LEARN * grad) * lax.rsqrt(state + EPS)

    for u in range(user_tiles):
        ustate_row[u:u + 1, :] = ustate[u * tile:(u + 1) * tile, :].T[0:1, :]

    def arrival(buf, axis, index, send, recv):
        return pltpu.make_async_remote_copy(
            src_ref=buf.at[index], dst_ref=buf.at[index], send_sem=send.at[0],
            recv_sem=recv.at[index], device_id={axis: index}, device_id_type=MESH)

    for d in range(1, n_help):
        arrival(sums_help, "help", lax.rem(my_help + d, n_help), help_send, help_recv).wait_recv()
    total = sums_help[0]
    for j in range(1, n_help):
        total = total + sums_help[j]
    sums_blk[my_blk] = total
    blks = []
    for d in range(1, n_blk):
        blks.append(pltpu.make_async_remote_copy(
            src_ref=sums_blk.at[my_blk], dst_ref=sums_blk.at[my_blk],
            send_sem=blk_send.at[d], recv_sem=blk_recv.at[my_blk],
            device_id={"blk": lax.rem(my_blk + d, n_blk)}, device_id_type=MESH))
        blks[-1].start()

    for c in range(chunks):
        lo = c * CHUNK
        code, aux = shift(strata - 1, c)
        code.wait_recv()
        aux.wait_recv()
        block = codes_in[strata - 1, c].astype(jnp.int32).astype(F32) * aux_in[strata - 1, c, 0:1, :]
        istate[0:1, lo:lo + CHUNK] = aux_in[strata - 1, c, 1:2, :]
        for k in range(per_chunk):
            items_nat[lo + k * tile:lo + (k + 1) * tile, :] = block[:, k * tile:(k + 1) * tile].T

    for d in range(1, n_blk):
        arrival(sums_blk, "blk", lax.rem(my_blk + d, n_blk), blk_send, blk_recv).wait_recv()
    total = sums_blk[0]
    for j in range(1, n_blk):
        total = total + sums_blk[j]
    loss_ref[...] = jnp.broadcast_to(
        jnp.sum(total[0:1, :], axis=1, keepdims=True) / jnp.sum(total[1:2, :], axis=1, keepdims=True), (1, tile))

    for copy in helps + blks:
        copy.wait_send()
    for hop in range(strata):
        for c in range(chunks):
            for copy in shift(hop, c):
                copy.wait_send()


def deliver(users, items, ustate, istate, loss, users_out, items_out, ustate_out, istate_out, loss_out, scalar, sems):
    scalar[0] = loss[0, 0]
    pairs = ((users, users_out), (items, items_out), (ustate, ustate_out), (istate, istate_out), (scalar, loss_out))
    copies = [pltpu.make_async_copy(src, dst, sems.at[n]) for n, (src, dst) in enumerate(pairs)]
    for copy in copies:
        copy.start()
    for copy in copies:
        copy.wait()


def on_device(users, items, user_state, item_state, ratings, masks, tile_cells, tile_count):
    strata, capacity, tile = ratings.shape[2], ratings.shape[3], ratings.shape[4]
    rank = users.shape[1]
    n_users, n_items = users.shape[0], items.shape[0]
    user_tiles, item_tiles = n_users // tile, n_items // tile
    n_blk, n_help = lax.axis_size("blk"), lax.axis_size("help")
    chunks = n_items // CHUNK
    sizes = (strata, capacity, tile, rank, user_tiles, item_tiles, n_blk, n_help)
    hbm = pl.BlockSpec(memory_space=pl.ANY)
    smem = pl.BlockSpec(memory_space=pltpu.SMEM)
    vmem = pl.BlockSpec(memory_space=pltpu.VMEM)
    dma = pltpu.SemaphoreType.DMA
    outs = pl.pallas_call(
        functools.partial(kernel, sizes),
        out_shape=(
            pltpu.VMEM(users.shape, F32),
            pltpu.VMEM(items.shape, F32),
            pltpu.VMEM((user_tiles, tile), F32),
            pltpu.VMEM((1, n_items), F32),
            pltpu.VMEM((1, tile), F32),
        ),
        in_specs=[smem] + [hbm] * 6,
        out_specs=(vmem,) * 5,
        scratch_shapes=[
            pltpu.VMEM((rank, n_items), F32),
            pltpu.VMEM((user_tiles, tile), F32),
            pltpu.VMEM((n_users, tile), F32),
            pltpu.VMEM((n_users, n_items), BF16),
            pltpu.VMEM((n_items, rank), BF16),
            pltpu.VMEM((strata, chunks, rank, CHUNK), jnp.int16),
            pltpu.VMEM((strata, chunks, 8, CHUNK), F32),
            pltpu.VMEM((strata, chunks, rank, CHUNK), jnp.int16),
            pltpu.VMEM((strata, chunks, 8, CHUNK), F32),
            pltpu.VMEM((n_help, 8, tile), F32),
            pltpu.VMEM((n_blk, 8, tile), F32),
            dma((4 + 2 * strata,)),
            dma((strata, chunks)), dma((strata, chunks)),
            dma((strata, chunks)), dma((strata, chunks)),
            dma((n_help,)), dma((n_help,)),
            dma((n_blk,)), dma((n_blk,)),
        ] + [pltpu.VMEM((capacity, tile, tile), BF16)] * (2 * strata),
        compiler_params=pltpu.CompilerParams(
            collective_id=0, has_side_effects=True, vmem_limit_bytes=VMEM
        ),
        name="block_steps",
    )(tile_cells, users, items, user_state.reshape(user_tiles, tile), item_state.reshape(1, n_items), ratings, masks)
    outs = pl.pallas_call(
        deliver,
        out_shape=[jax.ShapeDtypeStruct(out.shape, F32) for out in outs[:4]] + [jax.ShapeDtypeStruct((1,), F32)],
        in_specs=[vmem] * 5,
        out_specs=[hbm] * 5,
        scratch_shapes=[pltpu.SMEM((1,), F32), dma((5,))],
        compiler_params=pltpu.CompilerParams(vmem_limit_bytes=4 * 1024 * 1024),
        name="deliver",
    )(*outs)
    users_out, items_out, ustate_out, istate_out, loss = outs
    return users_out, items_out, ustate_out.reshape(n_users), istate_out.reshape(n_items), loss


def solution(mesh):
    in_specs = (
        P(("groups", "blk", "help"), None),
        P(("groups", "blk", "help"), None),
        P(("groups", "blk", "help")),
        P(("groups", "blk", "help")),
        P(("groups", "blk"), "help", None, None, None, None),
        P(("groups", "blk"), "help", None, None, None, None),
        P(("groups", "blk"), "help", None, None),
        P(("groups", "blk"), "help", None),
    )
    out_specs = (
        P(("groups", "blk", "help"), None),
        P(("groups", "blk", "help"), None),
        P(("groups", "blk", "help")),
        P(("groups", "blk", "help")),
        P("groups"),
    )
    return jax.shard_map(
        on_device, mesh=mesh, in_specs=in_specs, out_specs=out_specs, check_vma=False
    )
```

```python
import functools

import jax
import jax.numpy as jnp
from jax import lax
from jax.experimental import pallas as pl
from jax.experimental.pallas import tpu as pltpu
from jax.sharding import PartitionSpec as P

INNER = 2
EPS = 1e-06
LEARN = 0.03
DECAY = 0.02
LEVELS = 32767.0
CHUNK = 256
VMEM = 56 * 1024 * 1024
MESH = pl.DeviceIdType.MESH
F32 = jnp.float32
BF16 = jnp.bfloat16


def inverse_cells(cells_ref, stratum, capacity):
    picked = [cells_ref[0, 0, stratum, slot] for slot in range(capacity)]
    where = []
    for cell in range(capacity):
        found = jnp.int32(0)
        for slot in range(1, capacity):
            found = jnp.where(picked[slot] == cell, jnp.int32(slot), found)
        where.append(found)
    return where


def encode(values):
    top = jnp.max(jnp.abs(values), axis=0, keepdims=True)
    scale = jnp.maximum(top, 1e-30) * (1.0 / LEVELS)
    codes = jnp.round(values * (1.0 / scale)).astype(jnp.int32).astype(jnp.int16)
    return codes, scale


def kernel(
    sizes,
    cells_ref, users_ref, items_ref, ustate_ref, istate_ref, ratings_ref, masks_ref,
    users, items_nat, ustate_row, istate, loss_ref,
    items, ustate_in, ustate, error,
    items_back, codes_out, aux_out, codes_in, aux_in, sums_help, sums_blk,
    load_sem, code_send, code_recv, aux_send, aux_recv,
    help_send, help_recv, blk_send, blk_recv, *tiles,
):
    strata, capacity, tile, rank, user_tiles, item_tiles, n_blk, n_help = sizes
    rat, msk = tiles[:strata], tiles[strata:]
    n_items = item_tiles * tile
    chunks = n_items // CHUNK
    per_chunk = CHUNK // tile
    my_blk = lax.axis_index("blk")
    my_help = lax.axis_index("help")
    right = lax.rem(my_blk + 1, n_blk)

    loads = {}
    plan = [("users", users_ref, users), ("items", items_ref, items_nat),
            ("ustate", ustate_ref, ustate_in), ("istate", istate_ref, istate)]
    for s in range(strata):
        plan.append((("m", s), masks_ref.at[0, 0, s], msk[s]))
        plan.append((("r", s), ratings_ref.at[0, 0, s], rat[s]))
    for number, (name, src, dst) in enumerate(plan):
        loads[name] = pltpu.make_async_copy(src, dst, load_sem.at[number])
        loads[name].start()

    barrier = pltpu.get_barrier_semaphore()
    for d in range(1, n_blk):
        pl.semaphore_signal(barrier, inc=1, device_id={"blk": lax.rem(my_blk + d, n_blk)}, device_id_type=MESH)
    for d in range(1, n_help):
        pl.semaphore_signal(barrier, inc=1, device_id={"help": lax.rem(my_help + d, n_help)}, device_id_type=MESH)

    slots = [inverse_cells(cells_ref, 0, capacity)]

    loads["items"].wait()
    for i in range(item_tiles):
        items[:, i * tile:(i + 1) * tile] = items_nat[i * tile:(i + 1) * tile, :].T
    loads["istate"].wait()
    loads["ustate"].wait()
    for u in range(user_tiles):
        ustate[u * tile:(u + 1) * tile, :] = jnp.broadcast_to(ustate_in[u:u + 1, :], (tile, tile)).T
    loads["users"].wait()

    squared = jnp.zeros((8, tile), F32)
    counted = jnp.zeros((8, tile), F32)

    def shift(hop, c):
        cols = pl.ds(c * CHUNK, CHUNK)
        code = pltpu.make_async_remote_copy(
            src_ref=codes_out.at[hop, c], dst_ref=codes_in.at[hop, c],
            send_sem=code_send.at[hop, c], recv_sem=code_recv.at[hop, c],
            device_id={"blk": right}, device_id_type=MESH)
        aux = pltpu.make_async_remote_copy(
            src_ref=aux_out.at[hop, c], dst_ref=aux_in.at[hop, c],
            send_sem=aux_send.at[hop, c], recv_sem=aux_recv.at[hop, c],
            device_id={"blk": right}, device_id_type=MESH)
        return code, aux

    def fold(x):
        return x.reshape(-1, 8, tile).sum(axis=0)

    for s in range(strata):
        if s > 0:
            slots.append(inverse_cells(cells_ref, s, capacity))
        loads[("m", s)].wait()
        loads[("r", s)].wait()
        for inner in range(INNER):
            last = inner == INNER - 1
            un = [users[u * tile:(u + 1) * tile, :].astype(BF16) for u in range(user_tiles)]
            ut = jnp.concatenate([x.T for x in un], axis=1)
            for c in range(chunks):
                lo, hi = c * CHUNK, (c + 1) * CHUNK
                if s > 0 and inner == 0:
                    code, aux = shift(s - 1, c)
                    code.wait_recv()
                    aux.wait_recv()
                    block = codes_in[s - 1, c].astype(jnp.int32).astype(F32) * aux_in[s - 1, c, 0:1, :]
                    items[:, lo:hi] = block
                    istate[0:1, lo:hi] = aux_in[s - 1, c, 1:2, :]
                block = items[:, lo:hi]
                narrow = block.astype(BF16)
                for k in range(per_chunk):
                    items_back[lo + k * tile:lo + (k + 1) * tile, :] = narrow[:, k * tile:(k + 1) * tile].T
                for u in range(user_tiles):
                    predicted = jnp.dot(un[u], narrow, preferred_element_type=F32)
                    for k in range(per_chunk):
                        i = c * per_chunk + k
                        at = slots[s][u * item_tiles + i]
                        weight = msk[s][at].astype(F32)
                        err = weight * (predicted[:, k * tile:(k + 1) * tile] - rat[s][at].astype(F32))
                        squared = squared + fold(err * err)
                        if inner == 0:
                            counted = counted + fold(weight)
                        error[u * tile:(u + 1) * tile, i * tile:(i + 1) * tile] = err.astype(BF16)
                if s == strata - 1 and last and c == chunks - 1:
                    mine = jnp.concatenate(
                        [jnp.sum(squared, axis=0, keepdims=True),
                         jnp.sum(counted, axis=0, keepdims=True) * float(INNER),
                         jnp.zeros((6, tile), F32)], axis=0)
                    sums_help[my_help] = mine
                    helps = []
                    for d in range(1, n_help):
                        helps.append(pltpu.make_async_remote_copy(
                            src_ref=sums_help.at[my_help], dst_ref=sums_help.at[my_help],
                            send_sem=help_send.at[d], recv_sem=help_recv.at[my_help],
                            device_id={"help": lax.rem(my_help + d, n_help)}, device_id_type=MESH))
                        helps[-1].start()
                grad = jnp.dot(ut, error[:, lo:hi], preferred_element_type=F32) + DECAY * block
                state = istate[0:1, lo:hi] + jnp.sum(grad * grad, axis=0, keepdims=True) * (1.0 / rank)
                block = block - (LEARN * grad) * lax.rsqrt(state + EPS)
                if not last:
                    items[:, lo:hi] = block
                    istate[0:1, lo:hi] = state
                else:
                    codes, scale = encode(block)
                    codes_out[s, c] = codes
                    aux_out[s, c] = jnp.concatenate([scale, state] + [jnp.zeros_like(scale)] * 6, axis=0)
                    if s == 0 and c == 0:
                        pl.semaphore_wait(barrier, (n_blk - 1) + (n_help - 1))
                    for copy in shift(s, c):
                        copy.start()
            for u in range(user_tiles):
                rows = slice(u * tile, (u + 1) * tile)
                own = users[rows, :]
                grad = jnp.dot(error[rows, :], items_back[...], preferred_element_type=F32) + DECAY * own
                state = ustate[rows, :] + jnp.sum(grad * grad, axis=1, keepdims=True) * (1.0 / rank)
                ustate[rows, :] = state
                users[rows, :] = own - (LEARN * grad) * lax.rsqrt(state + EPS)

    for u in range(user_tiles):
        ustate_row[u:u + 1, :] = ustate[u * tile:(u + 1) * tile, :].T[0:1, :]

    def arrival(buf, axis, index, send, recv):
        return pltpu.make_async_remote_copy(
            src_ref=buf.at[index], dst_ref=buf.at[index], send_sem=send.at[0],
            recv_sem=recv.at[index], device_id={axis: index}, device_id_type=MESH)

    for d in range(1, n_help):
        arrival(sums_help, "help", lax.rem(my_help + d, n_help), help_send, help_recv).wait_recv()
    total = sums_help[0]
    for j in range(1, n_help):
        total = total + sums_help[j]
    sums_blk[my_blk] = total
    blks = []
    for d in range(1, n_blk):
        blks.append(pltpu.make_async_remote_copy(
            src_ref=sums_blk.at[my_blk], dst_ref=sums_blk.at[my_blk],
            send_sem=blk_send.at[d], recv_sem=blk_recv.at[my_blk],
            device_id={"blk": lax.rem(my_blk + d, n_blk)}, device_id_type=MESH))
        blks[-1].start()

    for c in range(chunks):
        lo = c * CHUNK
        code, aux = shift(strata - 1, c)
        code.wait_recv()
        aux.wait_recv()
        block = codes_in[strata - 1, c].astype(jnp.int32).astype(F32) * aux_in[strata - 1, c, 0:1, :]
        istate[0:1, lo:lo + CHUNK] = aux_in[strata - 1, c, 1:2, :]
        for k in range(per_chunk):
            items_nat[lo + k * tile:lo + (k + 1) * tile, :] = block[:, k * tile:(k + 1) * tile].T

    for d in range(1, n_blk):
        arrival(sums_blk, "blk", lax.rem(my_blk + d, n_blk), blk_send, blk_recv).wait_recv()
    total = sums_blk[0]
    for j in range(1, n_blk):
        total = total + sums_blk[j]
    loss_ref[...] = jnp.broadcast_to(
        jnp.sum(total[0:1, :], axis=1, keepdims=True) / jnp.sum(total[1:2, :], axis=1, keepdims=True), (1, tile))

    for copy in helps + blks:
        copy.wait_send()
    for hop in range(strata):
        for c in range(chunks):
            for copy in shift(hop, c):
                copy.wait_send()


def deliver(users, items, ustate, istate, loss, users_out, items_out, ustate_out, istate_out, loss_out, scalar, sems):
    scalar[0] = loss[0, 0]
    pairs = ((users, users_out), (items, items_out), (ustate, ustate_out), (istate, istate_out), (scalar, loss_out))
    copies = [pltpu.make_async_copy(src, dst, sems.at[n]) for n, (src, dst) in enumerate(pairs)]
    for copy in copies:
        copy.start()
    for copy in copies:
        copy.wait()


def on_device(users, items, user_state, item_state, ratings, masks, tile_cells, tile_count):
    strata, capacity, tile = ratings.shape[2], ratings.shape[3], ratings.shape[4]
    rank = users.shape[1]
    n_users, n_items = users.shape[0], items.shape[0]
    user_tiles, item_tiles = n_users // tile, n_items // tile
    n_blk, n_help = lax.axis_size("blk"), lax.axis_size("help")
    chunks = n_items // CHUNK
    sizes = (strata, capacity, tile, rank, user_tiles, item_tiles, n_blk, n_help)
    hbm = pl.BlockSpec(memory_space=pl.ANY)
    smem = pl.BlockSpec(memory_space=pltpu.SMEM)
    vmem = pl.BlockSpec(memory_space=pltpu.VMEM)
    dma = pltpu.SemaphoreType.DMA
    outs = pl.pallas_call(
        functools.partial(kernel, sizes),
        out_shape=(
            pltpu.VMEM(users.shape, F32),
            pltpu.VMEM(items.shape, F32),
            pltpu.VMEM((user_tiles, tile), F32),
            pltpu.VMEM((1, n_items), F32),
            pltpu.VMEM((1, tile), F32),
        ),
        in_specs=[smem] + [hbm] * 6,
        out_specs=(vmem,) * 5,
        scratch_shapes=[
            pltpu.VMEM((rank, n_items), F32),
            pltpu.VMEM((user_tiles, tile), F32),
            pltpu.VMEM((n_users, tile), F32),
            pltpu.VMEM((n_users, n_items), BF16),
            pltpu.VMEM((n_items, rank), BF16),
            pltpu.VMEM((strata, chunks, rank, CHUNK), jnp.int16),
            pltpu.VMEM((strata, chunks, 8, CHUNK), F32),
            pltpu.VMEM((strata, chunks, rank, CHUNK), jnp.int16),
            pltpu.VMEM((strata, chunks, 8, CHUNK), F32),
            pltpu.VMEM((n_help, 8, tile), F32),
            pltpu.VMEM((n_blk, 8, tile), F32),
            dma((4 + 2 * strata,)),
            dma((strata, chunks)), dma((strata, chunks)),
            dma((strata, chunks)), dma((strata, chunks)),
            dma((n_help,)), dma((n_help,)),
            dma((n_blk,)), dma((n_blk,)),
        ] + [pltpu.VMEM((capacity, tile, tile), BF16)] * (2 * strata),
        compiler_params=pltpu.CompilerParams(
            collective_id=0, has_side_effects=True, vmem_limit_bytes=VMEM
        ),
        name="block_steps",
    )(tile_cells, users, items, user_state.reshape(user_tiles, tile), item_state.reshape(1, n_items), ratings, masks)
    outs = pl.pallas_call(
        deliver,
        out_shape=[jax.ShapeDtypeStruct(out.shape, F32) for out in outs[:4]] + [jax.ShapeDtypeStruct((1,), F32)],
        in_specs=[vmem] * 5,
        out_specs=[hbm] * 5,
        scratch_shapes=[pltpu.SMEM((1,), F32), dma((5,))],
        compiler_params=pltpu.CompilerParams(vmem_limit_bytes=4 * 1024 * 1024),
        name="deliver",
    )(*outs)
    users_out, items_out, ustate_out, istate_out, loss = outs
    return users_out, items_out, ustate_out.reshape(n_users), istate_out.reshape(n_items), loss


def solution(mesh):
    in_specs = (
        P(("groups", "blk", "help"), None),
        P(("groups", "blk", "help"), None),
        P(("groups", "blk", "help")),
        P(("groups", "blk", "help")),
        P(("groups", "blk"), "help", None, None, None, None),
        P(("groups", "blk"), "help", None, None, None, None),
        P(("groups", "blk"), "help", None, None),
        P(("groups", "blk"), "help", None),
    )
    out_specs = (
        P(("groups", "blk", "help"), None),
        P(("groups", "blk", "help"), None),
        P(("groups", "blk", "help")),
        P(("groups", "blk", "help")),
        P("groups"),
    )
    return jax.shard_map(
        on_device, mesh=mesh, in_specs=in_specs, out_specs=out_specs, check_vma=False
    )
```
